32 devices in a mesh: row: 8 (over z, y), col: 4 (over x, core).
Axes of the slice: x: 2, y: 2, z: 4, core: 2. Of those that a mesh axis runs over, the one named last changes fastest.
Arguments:
- s_rows: bfloat16 [8192, 256], P('row', 'col'), may hold values from -0.375 to 0.375
- iterate: bfloat16 [256, 32768], P('row', 'col'), may hold values from -6 to 6
Outputs:
- product: bfloat16 [8192, 32768], P('row', 'col')
The draws below stay inside these ranges and needn't reach their ends.
All inputs are finite; a program needn't handle non-finite values.
Results may differ from the reference program's by a relative error of at most 0.001.
Values may be sent and summed in bfloat16 or wider, within the bound.
A program may use at most 64 MiB of HBM per device.

```python
import jax
import jax.numpy as jnp
from jax import lax

N = 32768
M = 8192
K = 256


def level_of(own_key, shape, cuts, low, high):
    factor_of, own = 1.0, jax.random.fold_in(own_key, 6)
    for axis_at, shards_of in cuts:
        steps = jnp.exp(jax.random.uniform(jax.random.fold_in(own, axis_at), (shards_of,), jnp.float32, low / len(cuts), high / len(cuts)))
        factor_of = factor_of * jnp.repeat(steps, shape[axis_at] // shards_of).reshape([-1 if axis == axis_at else 1 for axis in range(len(shape))])
    return factor_of


def noise(stream_key, dims, scale, limit, pieces=(), held_as=jnp.bfloat16):
    level = level_of(stream_key, dims, pieces, -0.22, 0.18) if pieces else 1.0
    values = jax.random.normal(stream_key, dims, jnp.float32) * scale * level
    return jnp.minimum(jnp.maximum(values, -limit), limit).astype(held_as)


def setup_inputs(seed: int = 0) -> dict:
    seeds = jax.random.split(jax.random.key(seed), 3)
    return {
        "s_rows": noise(seeds[0], (M, K), K ** -0.5, 0.375, ((0, 8), (1, 4))),
        "iterate": noise(seeds[1], (K, N), 1.0, 6.0, ((0, 8), (1, 4))),
    }


def reference(s_rows, iterate):
    total = jnp.dot(s_rows.astype(jnp.float32), iterate.astype(jnp.float32), precision=lax.Precision.HIGHEST, preferred_element_type=jnp.float32)
    return total.astype(jnp.bfloat16)
```

```python
import functools

import jax
import jax.numpy as jnp
from jax import lax
from jax.experimental import pallas as pl
from jax.experimental.pallas import tpu as pltpu
from jax.sharding import PartitionSpec as P

MESH = pl.DeviceIdType.MESH
CHUNKS = 8
LINE = 4
TILE = 1024


def gather_kernel(st_ref, it_ref, s_ref, whole_ref, st_all, zsend, ysend, xsend, recv, s_send, s_recv, local):
    row, col = lax.axis_index("row"), lax.axis_index("col")
    z, y = row // 2, row % 2
    other = row + 1 - 2 * y
    pair = z + 1 - 2 * (z % 2)
    depth, columns = it_ref.shape
    width = columns // CHUNKS
    half = CHUNKS // 2
    kdepth = st_ref.shape[0]
    below, above = z > 0, z < LINE - 1

    def block(zz, yy, c):
        return (
            pl.ds(pl.multiple_of((2 * zz + yy) * depth, depth), depth),
            pl.ds(pl.multiple_of(c * width, width), width),
        )

    def own(c):
        return it_ref.at[:, pl.ds(pl.multiple_of(c * width, width), width)]

    def send(src, zz, yy, c, sem, target):
        return pltpu.make_async_remote_copy(
            src_ref=src,
            dst_ref=whole_ref.at[block(zz, yy, c)],
            send_sem=sem,
            recv_sem=recv.at[2 * zz + yy, c],
            device_id={"row": target},
            device_id_type=MESH,
        )

    def held(zz, yy, c):
        return whole_ref.at[block(zz, yy, c)]

    def down(src, zz, c):
        return send(src, zz, y, c, zsend.at[0, zz, c], row - 2)

    def up(src, zz, c):
        return send(src, zz, y, c, zsend.at[1, zz, c], row + 2)

    def across(src, zz, c):
        return send(src, zz, y, c, ysend.at[zz, c], other)

    def extra(c):
        return send(held(z, 1 - y, c), z, 1 - y, c, xsend.at[c], 2 * pair + y)

    def s_copy(k):
        far = (col // 2 + k // 2) % 2 * 2 + (col + k) % 2
        at = pl.ds(pl.multiple_of(col * kdepth, kdepth), kdepth)
        return pltpu.make_async_remote_copy(
            src_ref=st_ref,
            dst_ref=st_all.at[at],
            send_sem=s_send.at[k - 1],
            recv_sem=s_recv.at[k - 1],
            device_id={"col": far},
            device_id_type=MESH,
        )

    def arrived(zz, yy, c):
        pltpu.make_async_copy(held(zz, yy, c), held(zz, yy, c), recv.at[2 * zz + yy, c]).wait()

    mine = pltpu.make_async_copy(it_ref, whole_ref.at[pl.ds(pl.multiple_of(row * depth, depth), depth)], local.at[0])
    mine.start()
    mine_s = pltpu.make_async_copy(st_ref, st_all.at[pl.ds(pl.multiple_of(col * kdepth, kdepth), kdepth)], local.at[1])
    mine_s.start()

    barrier = pltpu.get_barrier_semaphore()

    @pl.when(below)
    def _():
        pl.semaphore_signal(barrier, inc=1, device_id={"row": row - 2}, device_id_type=MESH)

    @pl.when(above)
    def _():
        pl.semaphore_signal(barrier, inc=1, device_id={"row": row + 2}, device_id_type=MESH)

    pl.semaphore_signal(barrier, inc=1, device_id={"row": other}, device_id_type=MESH)
    for k in range(1, 4):
        far = (col // 2 + k // 2) % 2 * 2 + (col + k) % 2
        pl.semaphore_signal(barrier, inc=1, device_id={"col": far}, device_id_type=MESH)
    pl.semaphore_wait(barrier, 4 + below.astype(jnp.int32) + above.astype(jnp.int32))

    @pl.loop(0, CHUNKS)
    def _(c):
        @pl.when(below)
        def _():
            down(own(c), z, c).start()

        @pl.when(above)
        def _():
            up(own(c), z, c).start()

        across(own(c), z, c).start()

    for k in range(1, 4):
        s_copy(k).start()

    def pass_on(d):
        @pl.loop(0, CHUNKS)
        def _(c):
            for sign in (1, -1):
                zz = z + sign * d

                @pl.when((zz >= 0) & (zz < LINE))
                def _():
                    arrived(zz, y, c)
                    src = held(zz, y, c)

                    @pl.when(below if sign == 1 else above)
                    def _():
                        (down if sign == 1 else up)(src, zz, c).start()

                    @pl.when((zz != pair) | (c < half))
                    def _():
                        across(src, zz, c).start()

    pass_on(1)
    for k in range(1, 4):
        s_copy(k).wait_recv()
    mine_s.wait()
    s_ref[...] = st_all[...].T
    pass_on(2)

    @pl.loop(half, CHUNKS)
    def _(c):
        arrived(z, 1 - y, c)
        extra(c).start()

    pass_on(3)

    @pl.loop(0, CHUNKS)
    def _(c):
        for zz in range(LINE):
            @pl.when((zz != z) | (c < half))
            def _():
                arrived(zz, 1 - y, c)

    @pl.loop(0, CHUNKS)
    def _(c):
        for zz in range(LINE):
            @pl.when(below & (zz >= z))
            def _():
                down(own(c), zz, c).wait_send()

            @pl.when(above & (zz <= z))
            def _():
                up(own(c), zz, c).wait_send()

            @pl.when((zz != pair) | (c < half))
            def _():
                across(own(c), zz, c).wait_send()

        @pl.when(c >= half)
        def _():
            extra(c).wait_send()

    for k in range(1, 4):
        s_copy(k).wait_send()
    mine.wait()


def product_kernel(s_ref, w_ref, o_ref):
    o_ref[...] = jnp.dot(s_ref[...], w_ref[...], preferred_element_type=jnp.float32).astype(o_ref.dtype)


def gathered(s_rows, iterate):
    rows, part = s_rows.shape
    depth, columns = iterate.shape
    blocks = 2 * LINE
    dma = pltpu.SemaphoreType.DMA
    s, whole = pl.pallas_call(
        gather_kernel,
        out_shape=(
            jax.ShapeDtypeStruct((rows, 4 * part), s_rows.dtype),
            jax.ShapeDtypeStruct((blocks * depth, columns), iterate.dtype),
        ),
        in_specs=[pl.BlockSpec(memory_space=pl.ANY)] * 2,
        out_specs=(pl.BlockSpec(memory_space=pltpu.VMEM), pl.BlockSpec(memory_space=pl.ANY)),
        scratch_shapes=[
            pltpu.VMEM((4 * part, rows), s_rows.dtype),
            dma((2, LINE, CHUNKS)),
            dma((LINE, CHUNKS)),
            dma((CHUNKS,)),
            dma((blocks, CHUNKS)),
            dma((3,)),
            dma((3,)),
            dma((2,)),
        ],
        compiler_params=pltpu.CompilerParams(collective_id=0, has_side_effects=True),
    )(s_rows.T, iterate)
    return pl.pallas_call(
        product_kernel,
        grid=(columns // TILE,),
        in_specs=[
            pl.BlockSpec(s.shape, lambda j: (0, 0)),
            pl.BlockSpec((whole.shape[0], TILE), lambda j: (0, j)),
        ],
        out_specs=pl.BlockSpec((rows, TILE), lambda j: (0, j)),
        out_shape=jax.ShapeDtypeStruct((rows, columns), jnp.bfloat16),
        compiler_params=pltpu.CompilerParams(vmem_limit_bytes=60 << 20),
    )(s, whole)


def shards(s_rows, iterate):
    panel_rows = lax.all_gather(s_rows, "col", axis=1, tiled=True)
    whole = lax.all_gather(iterate, "row", axis=0, tiled=True)
    product = jnp.dot(panel_rows, whole, preferred_element_type=jnp.float32)
    return product.astype(jnp.bfloat16)


def solution(mesh):
    small = mesh.shape["row"] == 2 * LINE and mesh.shape["col"] == 4
    return jax.shard_map(
        gathered if small else shards,
        mesh=mesh,
        in_specs=(P("row", "col"), P("row", "col")),
        out_specs=P("row", "col"),
        check_vma=False,
    )
```

```python
import functools

import jax
import jax.numpy as jnp
from jax import lax
from jax.experimental import pallas as pl
from jax.experimental.pallas import tpu as pltpu
from jax.sharding import PartitionSpec as P

MESH = pl.DeviceIdType.MESH
CHUNKS = 8
LINE = 4
LAG = 4


def gather_kernel(st_ref, it_ref, o_ref, whole_ref, s, st_all, zsend, ysend, xsend, recv, s_send, s_recv, local):
    row, col = lax.axis_index("row"), lax.axis_index("col")
    z, y = row // 2, row % 2
    other = row + 1 - 2 * y
    pair = z + 1 - 2 * (z % 2)
    depth, columns = it_ref.shape
    width = columns // CHUNKS
    half = CHUNKS // 2
    kdepth = st_ref.shape[0]
    below, above = z > 0, z < LINE - 1

    def block(zz, yy, c):
        return (
            pl.ds(pl.multiple_of((2 * zz + yy) * depth, depth), depth),
            pl.ds(pl.multiple_of(c * width, width), width),
        )

    def own(c):
        return it_ref.at[:, pl.ds(pl.multiple_of(c * width, width), width)]

    def send(src, zz, yy, c, sem, target):
        return pltpu.make_async_remote_copy(
            src_ref=src,
            dst_ref=whole_ref.at[block(zz, yy, c)],
            send_sem=sem,
            recv_sem=recv.at[2 * zz + yy, c],
            device_id={"row": target},
            device_id_type=MESH,
        )

    def held(zz, yy, c):
        return whole_ref.at[block(zz, yy, c)]

    def down(src, zz, c):
        return send(src, zz, y, c, zsend.at[0, zz, c], row - 2)

    def up(src, zz, c):
        return send(src, zz, y, c, zsend.at[1, zz, c], row + 2)

    def across(src, zz, c):
        return send(src, zz, y, c, ysend.at[zz, c], other)

    def extra(c):
        return send(held(z, 1 - y, c), z, 1 - y, c, xsend.at[c], 2 * pair + y)

    def s_copy(k):
        far = (col // 2 + k // 2) % 2 * 2 + (col + k) % 2
        at = pl.ds(pl.multiple_of(col * kdepth, kdepth), kdepth)
        return pltpu.make_async_remote_copy(
            src_ref=st_ref,
            dst_ref=st_all.at[at],
            send_sem=s_send.at[k - 1],
            recv_sem=s_recv.at[k - 1],
            device_id={"col": far},
            device_id_type=MESH,
        )

    def arrived(zz, yy, c):
        pltpu.make_async_copy(held(zz, yy, c), held(zz, yy, c), recv.at[2 * zz + yy, c]).wait()

    mine = pltpu.make_async_copy(it_ref, whole_ref.at[pl.ds(pl.multiple_of(row * depth, depth), depth)], local.at[0])
    mine.start()
    mine_s = pltpu.make_async_copy(st_ref, st_all.at[pl.ds(pl.multiple_of(col * kdepth, kdepth), kdepth)], local.at[1])
    mine_s.start()

    barrier = pltpu.get_barrier_semaphore()

    @pl.when(below)
    def _():
        pl.semaphore_signal(barrier, inc=1, device_id={"row": row - 2}, device_id_type=MESH)

    @pl.when(above)
    def _():
        pl.semaphore_signal(barrier, inc=1, device_id={"row": row + 2}, device_id_type=MESH)

    pl.semaphore_signal(barrier, inc=1, device_id={"row": other}, device_id_type=MESH)
    for k in range(1, 4):
        far = (col // 2 + k // 2) % 2 * 2 + (col + k) % 2
        pl.semaphore_signal(barrier, inc=1, device_id={"col": far}, device_id_type=MESH)
    pl.semaphore_wait(barrier, 4 + below.astype(jnp.int32) + above.astype(jnp.int32))

    @pl.loop(0, CHUNKS)
    def _(c):
        @pl.when(below)
        def _():
            down(own(c), z, c).start()

        @pl.when(above)
        def _():
            up(own(c), z, c).start()

        across(own(c), z, c).start()

    for k in range(1, 4):
        s_copy(k).start()
    for k in range(1, 4):
        s_copy(k).wait_recv()
    mine_s.wait()
    s[...] = st_all[...].T
    mine.wait()

    def pass_on(d, c):
        for sign in (1, -1):
            zz = z + sign * d

            @pl.when((zz >= 0) & (zz < LINE))
            def _():
                arrived(zz, y, c)
                src = held(zz, y, c)

                @pl.when(below if sign == 1 else above)
                def _():
                    (down if sign == 1 else up)(src, zz, c).start()

                @pl.when((zz != pair) | (c < half))
                def _():
                    across(src, zz, c).start()

    def multiply(c):
        for zz in range(LINE):
            @pl.when((zz != z) | (c < half))
            def _():
                arrived(zz, 1 - y, c)

        w = whole_ref[:, pl.ds(pl.multiple_of(c * width, width), width)]
        o_ref[c] = jnp.dot(s[...], w, preferred_element_type=jnp.float32).astype(o_ref.dtype)

    @pl.loop(0, CHUNKS + LAG)
    def _(t):
        @pl.when(t < CHUNKS)
        def _():
            pass_on(1, t)

        for d in (2, 3):
            @pl.when((t >= d - 1) & (t < CHUNKS + d - 1))
            def _():
                pass_on(d, t - d + 1)

        @pl.when((t >= half + 2) & (t < CHUNKS + 2))
        def _():
            arrived(z, 1 - y, t - 2)
            extra(t - 2).start()

        @pl.when(t >= LAG)
        def _():
            multiply(t - LAG)

    @pl.loop(0, CHUNKS)
    def _(c):
        for zz in range(LINE):
            @pl.when(below & (zz >= z))
            def _():
                down(own(c), zz, c).wait_send()

            @pl.when(above & (zz <= z))
            def _():
                up(own(c), zz, c).wait_send()

            @pl.when((zz != pair) | (c < half))
            def _():
                across(own(c), zz, c).wait_send()

        @pl.when(c >= half)
        def _():
            extra(c).wait_send()

    for k in range(1, 4):
        s_copy(k).wait_send()


def write_kernel(part_ref, out_ref, sems):
    chunks, _, width = part_ref.shape
    copies = [
        pltpu.make_async_copy(part_ref.at[c], out_ref.at[:, c * width : (c + 1) * width], sems.at[c])
        for c in range(chunks)
    ]
    for copy in copies:
        copy.start()
    for copy in copies:
        copy.wait()


def gathered(s_rows, iterate):
    rows, part = s_rows.shape
    depth, columns = iterate.shape
    blocks, width = 2 * LINE, columns // CHUNKS
    dma = pltpu.SemaphoreType.DMA
    product = pl.pallas_call(
        gather_kernel,
        out_shape=pltpu.VMEM((CHUNKS, rows, width), jnp.bfloat16),
        in_specs=[pl.BlockSpec(memory_space=pl.ANY)] * 2,
        out_specs=pl.BlockSpec(memory_space=pltpu.VMEM),
        scratch_shapes=[
            pltpu.VMEM((blocks * depth, columns), iterate.dtype),
            pltpu.VMEM((rows, 4 * part), s_rows.dtype),
            pltpu.VMEM((4 * part, rows), s_rows.dtype),
            dma((2, LINE, CHUNKS)),
            dma((LINE, CHUNKS)),
            dma((CHUNKS,)),
            dma((blocks, CHUNKS)),
            dma((3,)),
            dma((3,)),
            dma((2,)),
        ],
        compiler_params=pltpu.CompilerParams(collective_id=0, has_side_effects=True, vmem_limit_bytes=44 << 20),
    )(s_rows.T, iterate)
    return pl.pallas_call(
        write_kernel,
        in_specs=[pl.BlockSpec(memory_space=pltpu.VMEM)],
        out_specs=pl.BlockSpec(memory_space=pl.ANY),
        out_shape=jax.ShapeDtypeStruct((rows, columns), jnp.bfloat16),
        scratch_shapes=[dma((CHUNKS,))],
        compiler_params=pltpu.CompilerParams(vmem_limit_bytes=24 << 20),
    )(product)


def shards(s_rows, iterate):
    panel_rows = lax.all_gather(s_rows, "col", axis=1, tiled=True)
    whole = lax.all_gather(iterate, "row", axis=0, tiled=True)
    product = jnp.dot(panel_rows, whole, preferred_element_type=jnp.float32)
    return product.astype(jnp.bfloat16)


def solution(mesh):
    small = mesh.shape["row"] == 2 * LINE and mesh.shape["col"] == 4
    return jax.shard_map(
        gathered if small else shards,
        mesh=mesh,
        in_specs=(P("row", "col"), P("row", "col")),
        out_specs=P("row", "col"),
        check_vma=False,
    )
```

```python
import functools

import jax
import jax.numpy as jnp
from jax import lax
from jax.experimental import pallas as pl
from jax.experimental.pallas import tpu as pltpu
from jax.sharding import PartitionSpec as P

MESH = pl.DeviceIdType.MESH
CHUNKS = 4
HOLD = 1
TILE = 512
LINE = 4
LAG = 3


def gather_kernel(st_ref, it_ref, o_ref, whole_ref, s, st_all, zsend, ysend, xsend, recv, s_send, s_recv, local):
    row, col = lax.axis_index("row"), lax.axis_index("col")
    z, y = row // 2, row % 2
    other = row + 1 - 2 * y
    pair = z + 1 - 2 * (z % 2)
    depth, columns = it_ref.shape
    width = columns // CHUNKS
    half = CHUNKS // 2
    kdepth = st_ref.shape[0]
    below, above = z > 0, z < LINE - 1

    def block(zz, yy, c):
        return (
            pl.ds(pl.multiple_of((2 * zz + yy) * depth, depth), depth),
            pl.ds(pl.multiple_of(c * width, width), width),
        )

    def own(c):
        return it_ref.at[:, pl.ds(pl.multiple_of(c * width, width), width)]

    def send(src, zz, yy, c, sem, target):
        return pltpu.make_async_remote_copy(
            src_ref=src,
            dst_ref=whole_ref.at[block(zz, yy, c)],
            send_sem=sem,
            recv_sem=recv.at[2 * zz + yy, c],
            device_id={"row": target},
            device_id_type=MESH,
        )

    def held(zz, yy, c):
        return whole_ref.at[block(zz, yy, c)]

    def down(src, zz, c):
        return send(src, zz, y, c, zsend.at[0, zz, c], row - 2)

    def up(src, zz, c):
        return send(src, zz, y, c, zsend.at[1, zz, c], row + 2)

    def across(src, zz, c):
        return send(src, zz, y, c, ysend.at[zz, c], other)

    def extra(c):
        return send(held(z, 1 - y, c), z, 1 - y, c, xsend.at[c], 2 * pair + y)

    def s_copy(k):
        far = (col // 2 + k // 2) % 2 * 2 + (col + k) % 2
        at = pl.ds(pl.multiple_of(col * kdepth, kdepth), kdepth)
        return pltpu.make_async_remote_copy(
            src_ref=st_ref,
            dst_ref=st_all.at[at],
            send_sem=s_send.at[k - 1],
            recv_sem=s_recv.at[k - 1],
            device_id={"col": far},
            device_id_type=MESH,
        )

    def arrived(zz, yy, c):
        pltpu.make_async_copy(held(zz, yy, c), held(zz, yy, c), recv.at[2 * zz + yy, c]).wait()

    mine = pltpu.make_async_copy(it_ref, whole_ref.at[pl.ds(pl.multiple_of(row * depth, depth), depth)], local.at[0])
    mine.start()
    mine_s = pltpu.make_async_copy(st_ref, st_all.at[pl.ds(pl.multiple_of(col * kdepth, kdepth), kdepth)], local.at[1])
    mine_s.start()

    barrier = pltpu.get_barrier_semaphore()

    @pl.when(below)
    def _():
        pl.semaphore_signal(barrier, inc=1, device_id={"row": row - 2}, device_id_type=MESH)

    @pl.when(above)
    def _():
        pl.semaphore_signal(barrier, inc=1, device_id={"row": row + 2}, device_id_type=MESH)

    pl.semaphore_signal(barrier, inc=1, device_id={"row": other}, device_id_type=MESH)
    for k in range(1, 4):
        far = (col // 2 + k // 2) % 2 * 2 + (col + k) % 2
        pl.semaphore_signal(barrier, inc=1, device_id={"col": far}, device_id_type=MESH)
    pl.semaphore_wait(barrier, 4 + below.astype(jnp.int32) + above.astype(jnp.int32))

    @pl.loop(0, CHUNKS)
    def _(c):
        @pl.when(below)
        def _():
            down(own(c), z, c).start()

        @pl.when(above)
        def _():
            up(own(c), z, c).start()

        across(own(c), z, c).start()

    for k in range(1, 4):
        s_copy(k).start()
    for k in range(1, 4):
        s_copy(k).wait_recv()
    mine_s.wait()
    s[...] = st_all[...].T
    mine.wait()

    def pass_on(d, c):
        for sign in (1, -1):
            zz = z + sign * d

            @pl.when((zz >= 0) & (zz < LINE))
            def _():
                arrived(zz, y, c)
                src = held(zz, y, c)

                @pl.when(below if sign == 1 else above)
                def _():
                    (down if sign == 1 else up)(src, zz, c).start()

                @pl.when((zz != pair) | (c < half))
                def _():
                    across(src, zz, c).start()

    def multiply(c):
        for zz in range(LINE):
            @pl.when((zz != z) | (c < half))
            def _():
                arrived(zz, 1 - y, c)

        @pl.when(c < CHUNKS - HOLD)
        def _():
            w = whole_ref[:, pl.ds(pl.multiple_of(c * width, width), width)]
            o_ref[c] = jnp.dot(s[...], w, preferred_element_type=jnp.float32).astype(o_ref.dtype)

    @pl.loop(0, CHUNKS + LAG)
    def _(t):
        @pl.when(t < CHUNKS)
        def _():
            pass_on(1, t)

        for d in (2, 3):
            @pl.when((t >= d - 1) & (t < CHUNKS + d - 1))
            def _():
                pass_on(d, t - d + 1)

        @pl.when((t >= half + 2) & (t < CHUNKS + 2))
        def _():
            arrived(z, 1 - y, t - 2)
            extra(t - 2).start()

        @pl.when(t >= LAG)
        def _():
            multiply(t - LAG)

    @pl.loop(0, CHUNKS)
    def _(c):
        for zz in range(LINE):
            @pl.when(below & (zz >= z))
            def _():
                down(own(c), zz, c).wait_send()

            @pl.when(above & (zz <= z))
            def _():
                up(own(c), zz, c).wait_send()

            @pl.when((zz != pair) | (c < half))
            def _():
                across(own(c), zz, c).wait_send()

        @pl.when(c >= half)
        def _():
            extra(c).wait_send()

    for k in range(1, 4):
        s_copy(k).wait_send()


def write_kernel(part_ref, whole_ref, s_ref, out_ref, late, sems, late_sems):
    chunks, _, width = part_ref.shape
    tiles, _, tile = late.shape
    copies = [
        pltpu.make_async_copy(part_ref.at[c], out_ref.at[:, c * width : (c + 1) * width], sems.at[c])
        for c in range(chunks)
    ]
    for copy in copies:
        copy.start()

    def at(t):
        return pl.ds(pl.multiple_of(chunks * width + t * tile, tile), tile)

    def tail(t):
        return pltpu.make_async_copy(late.at[t], out_ref.at[:, at(t)], late_sems.at[t])

    @pl.loop(0, tiles)
    def _(t):
        late[t] = jnp.dot(s_ref[...], whole_ref[:, at(t)], preferred_element_type=jnp.float32).astype(late.dtype)
        tail(t).start()

    for copy in copies:
        copy.wait()

    @pl.loop(0, tiles)
    def _(t):
        tail(t).wait()


def gathered(s_rows, iterate):
    rows, part = s_rows.shape
    depth, columns = iterate.shape
    blocks, width = 2 * LINE, columns // CHUNKS
    dma = pltpu.SemaphoreType.DMA
    tile = min(TILE, width)
    tiles = HOLD * width // tile
    vmem = pl.BlockSpec(memory_space=pltpu.VMEM)
    part, whole, s = pl.pallas_call(
        gather_kernel,
        out_shape=(
            pltpu.VMEM((CHUNKS - HOLD, rows, width), jnp.bfloat16),
            pltpu.VMEM((blocks * depth, columns), iterate.dtype),
            pltpu.VMEM((rows, 4 * part), s_rows.dtype),
        ),
        in_specs=[pl.BlockSpec(memory_space=pl.ANY)] * 2,
        out_specs=(vmem, vmem, vmem),
        scratch_shapes=[
            pltpu.VMEM((4 * part, rows), s_rows.dtype),
            dma((2, LINE, CHUNKS)),
            dma((LINE, CHUNKS)),
            dma((CHUNKS,)),
            dma((blocks, CHUNKS)),
            dma((3,)),
            dma((3,)),
            dma((2,)),
        ],
        compiler_params=pltpu.CompilerParams(collective_id=0, has_side_effects=True, vmem_limit_bytes=16 << 20),
    )(s_rows.T, iterate)
    return pl.pallas_call(
        write_kernel,
        in_specs=[vmem] * 3,
        out_specs=pl.BlockSpec(memory_space=pl.ANY),
        out_shape=jax.ShapeDtypeStruct((rows, columns), jnp.bfloat16),
        scratch_shapes=[pltpu.VMEM((tiles, rows, tile), jnp.bfloat16), dma((CHUNKS - HOLD,)), dma((tiles,))],
        compiler_params=pltpu.CompilerParams(vmem_limit_bytes=16 << 20),
    )(part, whole, s)


def shards(s_rows, iterate):
    panel_rows = lax.all_gather(s_rows, "col", axis=1, tiled=True)
    whole = lax.all_gather(iterate, "row", axis=0, tiled=True)
    product = jnp.dot(panel_rows, whole, preferred_element_type=jnp.float32)
    return product.astype(jnp.bfloat16)


def solution(mesh):
    small = mesh.shape["row"] == 2 * LINE and mesh.shape["col"] == 4
    return jax.shard_map(
        gathered if small else shards,
        mesh=mesh,
        in_specs=(P("row", "col"), P("row", "col")),
        out_specs=P("row", "col"),
        check_vma=False,
    )
```

```python
import functools

import jax
import jax.numpy as jnp
from jax import lax
from jax.experimental import pallas as pl
from jax.experimental.pallas import tpu as pltpu
from jax.sharding import PartitionSpec as P

MESH = pl.DeviceIdType.MESH
CHUNKS = 4
HOLD = 1
TILE = 512
LINE = 4
LAG = 3


def gather_kernel(st_ref, it_ref, o_ref, whole_ref, s, st_all, zsend, ysend, xsend, recv, s_send, s_recv, local):
    row, col = lax.axis_index("row"), lax.axis_index("col")
    z, y = row // 2, row % 2
    other = row + 1 - 2 * y
    pair = z + 1 - 2 * (z % 2)
    depth, columns = it_ref.shape
    width = columns // CHUNKS
    half = CHUNKS // 2
    kdepth = st_ref.shape[0]
    below, above = z > 0, z < LINE - 1

    def block(zz, yy, c):
        return (
            pl.ds(pl.multiple_of((2 * zz + yy) * depth, depth), depth),
            pl.ds(pl.multiple_of(c * width, width), width),
        )

    def own(c):
        return it_ref.at[:, pl.ds(pl.multiple_of(c * width, width), width)]

    def send(src, zz, yy, c, sem, target):
        return pltpu.make_async_remote_copy(
            src_ref=src,
            dst_ref=whole_ref.at[block(zz, yy, c)],
            send_sem=sem,
            recv_sem=recv.at[2 * zz + yy, c],
            device_id={"row": target},
            device_id_type=MESH,
        )

    def held(zz, yy, c):
        return whole_ref.at[block(zz, yy, c)]

    def down(src, zz, c):
        return send(src, zz, y, c, zsend.at[0, zz, c], row - 2)

    def up(src, zz, c):
        return send(src, zz, y, c, zsend.at[1, zz, c], row + 2)

    def across(src, zz, c):
        return send(src, zz, y, c, ysend.at[zz, c], other)

    def extra(c):
        return send(held(z, 1 - y, c), z, 1 - y, c, xsend.at[c], 2 * pair + y)

    def s_copy(k):
        far = (col // 2 + k // 2) % 2 * 2 + (col + k) % 2
        at = pl.ds(pl.multiple_of(col * kdepth, kdepth), kdepth)
        return pltpu.make_async_remote_copy(
            src_ref=st_ref,
            dst_ref=st_all.at[at],
            send_sem=s_send.at[k - 1],
            recv_sem=s_recv.at[k - 1],
            device_id={"col": far},
            device_id_type=MESH,
        )

    def arrived(zz, yy, c):
        pltpu.make_async_copy(held(zz, yy, c), held(zz, yy, c), recv.at[2 * zz + yy, c]).wait()

    mine = pltpu.make_async_copy(it_ref, whole_ref.at[pl.ds(pl.multiple_of(row * depth, depth), depth)], local.at[0])
    mine.start()
    mine_s = pltpu.make_async_copy(st_ref, st_all.at[pl.ds(pl.multiple_of(col * kdepth, kdepth), kdepth)], local.at[1])
    mine_s.start()

    barrier = pltpu.get_barrier_semaphore()

    @pl.when(below)
    def _():
        pl.semaphore_signal(barrier, inc=1, device_id={"row": row - 2}, device_id_type=MESH)

    @pl.when(above)
    def _():
        pl.semaphore_signal(barrier, inc=1, device_id={"row": row + 2}, device_id_type=MESH)

    pl.semaphore_signal(barrier, inc=1, device_id={"row": other}, device_id_type=MESH)
    for k in range(1, 4):
        far = (col // 2 + k // 2) % 2 * 2 + (col + k) % 2
        pl.semaphore_signal(barrier, inc=1, device_id={"col": far}, device_id_type=MESH)
    pl.semaphore_wait(barrier, 4 + below.astype(jnp.int32) + above.astype(jnp.int32))

    @pl.loop(0, CHUNKS)
    def _(c):
        @pl.when(below)
        def _():
            down(own(c), z, c).start()

        @pl.when(above)
        def _():
            up(own(c), z, c).start()

        across(own(c), z, c).start()

    for k in range(1, 4):
        s_copy(k).start()
    for k in range(1, 4):
        s_copy(k).wait_recv()
    mine_s.wait()
    s[...] = st_all[...].T
    mine.wait()

    def pass_on(d, c):
        for sign in (1, -1):
            zz = z + sign * d

            @pl.when((zz >= 0) & (zz < LINE))
            def _():
                arrived(zz, y, c)
                src = held(zz, y, c)

                @pl.when(below if sign == 1 else above)
                def _():
                    (down if sign == 1 else up)(src, zz, c).start()

                @pl.when((zz != pair) | (c < half))
                def _():
                    across(src, zz, c).start()

    def multiply(c):
        for zz in range(LINE):
            @pl.when((zz != z) | (c < half))
            def _():
                arrived(zz, 1 - y, c)

        @pl.when(c < CHUNKS - HOLD)
        def _():
            w = whole_ref[:, pl.ds(pl.multiple_of(c * width, width), width)]
            o_ref[c] = jnp.dot(s[...], w, preferred_element_type=jnp.float32).astype(o_ref.dtype)

    @pl.loop(0, CHUNKS + LAG)
    def _(t):
        @pl.when(t < CHUNKS)
        def _():
            pass_on(1, t)

        for d in (2, 3):
            @pl.when((t >= d - 1) & (t < CHUNKS + d - 1))
            def _():
                pass_on(d, t - d + 1)

        @pl.when((t >= half + 2) & (t < CHUNKS + 2))
        def _():
            arrived(z, 1 - y, t - 2)
            extra(t - 2).start()

        @pl.when(t >= LAG)
        def _():
            multiply(t - LAG)

    @pl.loop(0, CHUNKS)
    def _(c):
        for zz in range(LINE):
            @pl.when(below & (zz >= z))
            def _():
                down(own(c), zz, c).wait_send()

            @pl.when(above & (zz <= z))
            def _():
                up(own(c), zz, c).wait_send()

            @pl.when((zz != pair) | (c < half))
            def _():
                across(own(c), zz, c).wait_send()

        @pl.when(c >= half)
        def _():
            extra(c).wait_send()

    for k in range(1, 4):
        s_copy(k).wait_send()


def write_kernel(part_ref, whole_ref, s_ref, out_ref, late, sems, late_sems):
    chunks, _, width = part_ref.shape
    tiles, _, tile = late.shape
    copies = [
        pltpu.make_async_copy(part_ref.at[c], out_ref.at[:, c * width : (c + 1) * width], sems.at[c])
        for c in range(chunks)
    ]
    for copy in copies:
        copy.start()

    def at(t):
        return pl.ds(pl.multiple_of(chunks * width + t * tile, tile), tile)

    def tail(t):
        return pltpu.make_async_copy(late.at[t], out_ref.at[:, at(t)], late_sems.at[t])

    @pl.loop(0, tiles)
    def _(t):
        late[t] = jnp.dot(s_ref[...], whole_ref[:, at(t)], preferred_element_type=jnp.float32).astype(late.dtype)
        tail(t).start()

    for copy in copies:
        copy.wait()

    @pl.loop(0, tiles)
    def _(t):
        tail(t).wait()


def gathered(s_rows, iterate):
    rows, part = s_rows.shape
    depth, columns = iterate.shape
    blocks, width = 2 * LINE, columns // CHUNKS
    dma = pltpu.SemaphoreType.DMA
    tile = min(TILE, width)
    tiles = HOLD * width // tile
    vmem = pl.BlockSpec(memory_space=pltpu.VMEM)
    part, whole, s = pl.pallas_call(
        gather_kernel,
        out_shape=(
            pltpu.VMEM((CHUNKS - HOLD, rows, width), jnp.bfloat16),
            pltpu.VMEM((blocks * depth, columns), iterate.dtype),
            pltpu.VMEM((rows, 4 * part), s_rows.dtype),
        ),
        in_specs=[pl.BlockSpec(memory_space=pl.ANY)] * 2,
        out_specs=(vmem, vmem, vmem),
        scratch_shapes=[
            pltpu.VMEM((4 * part, rows), s_rows.dtype),
            dma((2, LINE, CHUNKS)),
            dma((LINE, CHUNKS)),
            dma((CHUNKS,)),
            dma((blocks, CHUNKS)),
            dma((3,)),
            dma((3,)),
            dma((2,)),
        ],
        compiler_params=pltpu.CompilerParams(collective_id=0, has_side_effects=True, vmem_limit_bytes=40 << 20),
    )(s_rows.T, iterate)
    return pl.pallas_call(
        write_kernel,
        in_specs=[vmem] * 3,
        out_specs=pl.BlockSpec(memory_space=pl.ANY),
        out_shape=jax.ShapeDtypeStruct((rows, columns), jnp.bfloat16),
        scratch_shapes=[pltpu.VMEM((tiles, rows, tile), jnp.bfloat16), dma((CHUNKS - HOLD,)), dma((tiles,))],
        compiler_params=pltpu.CompilerParams(vmem_limit_bytes=16 << 20),
    )(part, whole, s)


def shards(s_rows, iterate):
    panel_rows = lax.all_gather(s_rows, "col", axis=1, tiled=True)
    whole = lax.all_gather(iterate, "row", axis=0, tiled=True)
    product = jnp.dot(panel_rows, whole, preferred_element_type=jnp.float32)
    return product.astype(jnp.bfloat16)


def solution(mesh):
    small = mesh.shape["row"] == 2 * LINE and mesh.shape["col"] == 4
    return jax.shard_map(
        gathered if small else shards,
        mesh=mesh,
        in_specs=(P("row", "col"), P("row", "col")),
        out_specs=P("row", "col"),
        check_vma=False,
    )
```
